32 devices in a mesh: grp: 2 (over y), inner: 4 (over x, core), outer: 4 (over z).
Axes of the slice: x: 2, y: 2, z: 4, core: 2. Of those that a mesh axis runs over, the one named last changes fastest.
Arguments:
- queries: bfloat16 [8, 1024, 2048], P(('grp', 'outer'), 'inner'), parts along dimension 0, may hold values from -8 to 8
- keys: bfloat16 [8, 1024, 512], P(('grp', 'outer'), 'inner'), parts along dimension 0, may hold values from -5 to 5
- values: bfloat16 [8, 1024, 512], P(('grp', 'outer'), 'inner'), parts along dimension 0, may hold values from -6 to 6
- out_grad: bfloat16 [8, 1024, 2048], P(('grp', 'outer'), 'inner'), parts along dimension 0, may hold values from -6 to 6
- attn_out: bfloat16 [8, 1024, 2048], P(('grp', 'outer'), 'inner'), parts along dimension 0, may hold values from -6 to 6
- block_mask: int32 [8, 4, 3], P(('grp', 'outer'), 'inner'), parts along dimension 0, may hold values 0 or 1
- scale_exponents: int32 [8, 4, 8], P(('grp', 'outer'), 'inner'), parts along dimension 0, may hold values from -1 to 1
Outputs:
- query_grad: bfloat16 [8, 1024, 2048], P(('grp', 'outer'), 'inner'), parts along dimension 0
- key_grad: bfloat16 [8, 1024, 512], P(('grp', 'outer'), 'inner'), parts along dimension 0
- value_grad: bfloat16 [8, 1024, 512], P(('grp', 'outer'), 'inner'), parts along dimension 0
The draws below stay inside these ranges and needn't reach their ends.
There are 2 independent parts, one for each index of `grp`. The reference program is written for one: setup_inputs(seed, part) draws one part's arguments, and reference() takes and returns one part's arrays. A program takes and returns all parts, laid end to end along the dimension named above; each array names one. Nothing has to cross between parts.
All inputs are finite; a program needn't handle non-finite values. No bound on the sum of `block_mask` on one device may be relied on, other than what follows from the above.
Results may differ from the reference program's by a relative error of at most 0.005.
Values may be sent and summed in bfloat16 or wider, within the bound.
A program may use at most 64 MiB of HBM per device.

```python
import jax
import jax.numpy as jnp
from jax import lax

HEADS = 16
KV_HEADS = 4
HEAD_DIM = 128
STEPS = 4
TOK_DEV = 256
GROUP = 4
GROUPS = 4
GROUP_TOKENS = 1024
N_INNER = 4


def draw_keys(key, part):
    key = jax.random.fold_in(key, 11)
    shape = (GROUPS, GROUP_TOKENS, KV_HEADS, HEAD_DIM)
    base = jnp.clip(jax.random.normal(key, shape, jnp.float32), -5.0, 5.0)
    return base.reshape(GROUPS, GROUP_TOKENS, KV_HEADS * HEAD_DIM).astype(jnp.bfloat16)


def draw_queries(key, part):
    key = jax.random.fold_in(key, 13)
    shape = (GROUPS, GROUP_TOKENS, KV_HEADS, GROUP, HEAD_DIM)
    base = jnp.clip(2.0 * jax.random.normal(key, shape, jnp.float32), -8.0, 8.0)
    return base.reshape(GROUPS, GROUP_TOKENS, HEADS * HEAD_DIM).astype(jnp.bfloat16)


def with_ends(drawn, key, low, top_value):
    dims = drawn.shape
    index_at = [jax.random.randint(jax.random.fold_in(key, axis), (), 0, dims[axis]) for axis in range(len(dims))]
    drawn = drawn.at[tuple(index_at)].set(low)
    longest = dims.index(max(dims))
    index_at[longest] = (index_at[longest] + 1) % dims[longest]
    return drawn.at[tuple(index_at)].set(top_value)


def steps_of(key, dims, cuts, low, largest):
    level, own = 1.0, jax.random.fold_in(key, 6)
    for position, parts in cuts:
        draws = jnp.exp(jax.random.uniform(jax.random.fold_in(own, position), (parts,), jnp.float32, low / len(cuts), largest / len(cuts)))
        level = level * jnp.repeat(draws, dims[position] // parts).reshape([-1 if axis == position else 1 for axis in range(len(dims))])
    return level


def centred(rng, dims, scale, limit, shards=(), kind=jnp.bfloat16):
    gain = steps_of(rng, dims, shards, -0.22, 0.18) if shards else 1.0
    values = jax.random.normal(rng, dims, jnp.float32) * scale * gain
    return jnp.minimum(jnp.maximum(values, -limit), limit).astype(kind)


def setup_inputs(seed: int = 0, part: int = 0) -> dict:
    streams_of = jax.random.split(jax.random.key(seed), 8)
    part_keys = jax.random.split(jax.random.fold_in(streams_of[7], part), 8)
    queries = draw_queries(jax.random.fold_in(jax.random.fold_in(streams_of[7], part), 71), part)
    keys = draw_keys(jax.random.fold_in(jax.random.fold_in(streams_of[7], part), 71), part)
    values = centred(part_keys[2], (GROUPS, GROUP_TOKENS, KV_HEADS * HEAD_DIM), 1.0, 6.0, ((0, 4), (1, 4)))
    out_grad = centred(part_keys[3], (GROUPS, GROUP_TOKENS, HEADS * HEAD_DIM), 1.0, 6.0, ((0, 4), (1, 4)))
    attn_out = centred(part_keys[4], (GROUPS, GROUP_TOKENS, HEADS * HEAD_DIM), 1.0, 6.0, ((0, 4), (1, 4)))
    block_mask = with_ends((jax.random.randint(part_keys[5], (GROUPS, N_INNER, STEPS - 1), 0, 2) < 1).astype(jnp.int32), jax.random.fold_in(part_keys[5], 1), 0, 1)
    scale_exponents = with_ends(jax.random.randint(part_keys[6], (GROUPS, N_INNER, 2 * KV_HEADS), -1, 2), jax.random.fold_in(part_keys[6], 1), -1, 1).astype(jnp.int32)
    return dict(queries=queries, keys=keys, values=values, out_grad=out_grad, attn_out=attn_out, block_mask=block_mask, scale_exponents=scale_exponents)


def reference(queries, keys, values, out_grad, attn_out, block_mask, scale_exponents):
    block_count = GROUPS * N_INNER
    kv_width = KV_HEADS * HEAD_DIM
    group_size = HEADS // KV_HEADS
    score_scale = HEAD_DIM ** -0.5
    factors = jnp.exp2(scale_exponents.reshape(block_count, 2 * KV_HEADS).astype(jnp.float32))
    key_factor = jnp.repeat(factors[:, :KV_HEADS], HEAD_DIM, axis=1)
    value_factor = jnp.repeat(factors[:, KV_HEADS:], HEAD_DIM, axis=1)
    key_blocks = (keys.reshape(block_count, TOK_DEV, kv_width).astype(jnp.float32) * key_factor[:, None, :]).astype(jnp.bfloat16)
    value_blocks = (values.reshape(block_count, TOK_DEV, kv_width).astype(jnp.float32) * value_factor[:, None, :]).astype(jnp.bfloat16)
    query_blocks = queries.reshape(block_count, TOK_DEV, KV_HEADS, group_size, HEAD_DIM)
    grad_blocks = out_grad.reshape(block_count, TOK_DEV, KV_HEADS, group_size, HEAD_DIM)
    saved_blocks = attn_out.reshape(block_count, TOK_DEV, KV_HEADS, group_size, HEAD_DIM)
    mask_rows = block_mask.reshape(block_count, STEPS - 1)
    positions = jnp.arange(TOK_DEV)
    causal = positions[:, None] >= positions[None, :]

    def one_block(carry, index):
        key_sum, value_sum = carry
        query_heads = query_blocks[index].astype(jnp.float32)
        grad_heads = grad_blocks[index].astype(jnp.float32)
        row_delta = jnp.sum(grad_heads * saved_blocks[index].astype(jnp.float32), -1).transpose(1, 2, 0)
        score_list = []
        sources = []
        for s in range(STEPS):
            source = jnp.maximum(index - s, 0).astype(jnp.int32)
            if s == 0:
                keep = causal
            else:
                keep = jnp.broadcast_to((index >= s) & (mask_rows[index, s - 1] == 1), (TOK_DEV, TOK_DEV))
            key_part = key_blocks[source].reshape(TOK_DEV, KV_HEADS, HEAD_DIM).astype(jnp.float32)
            scores = jnp.einsum("tgqd,ugd->gqtu", query_heads, key_part) * score_scale
            score_list.append(jnp.where(keep, scores, -1e30))
            sources.append(source)
        lse = jax.nn.logsumexp(jnp.concatenate(score_list, -1), axis=-1)
        query_sum = jnp.zeros((TOK_DEV, KV_HEADS, group_size, HEAD_DIM), jnp.float32)
        for s in range(STEPS):
            source = sources[s]
            key_part = key_blocks[source].reshape(TOK_DEV, KV_HEADS, HEAD_DIM).astype(jnp.float32)
            value_part = value_blocks[source].reshape(TOK_DEV, KV_HEADS, HEAD_DIM).astype(jnp.float32)
            probs = jnp.exp(score_list[s] - lse[..., None])
            probs_low = probs.astype(jnp.bfloat16).astype(jnp.float32)
            dprobs = jnp.einsum("tgqd,ugd->gqtu", grad_heads, value_part)
            dscores = (probs * (dprobs - row_delta[..., None])).astype(jnp.bfloat16).astype(jnp.float32)
            query_sum = query_sum + jnp.einsum("gqtu,ugd->tgqd", dscores, key_part) * score_scale
            key_term = jnp.einsum("gqtu,tgqd->ugd", dscores, query_heads) * score_scale
            value_term = jnp.einsum("gqtu,tgqd->ugd", probs_low, grad_heads)
            key_sum = key_sum.at[source].add(key_term.reshape(TOK_DEV, kv_width))
            value_sum = value_sum.at[source].add(value_term.reshape(TOK_DEV, kv_width))
        query_out = query_sum.reshape(TOK_DEV, HEADS * HEAD_DIM).astype(jnp.bfloat16)
        return (key_sum, value_sum), query_out

    empty = jnp.zeros((block_count, TOK_DEV, kv_width), jnp.float32)
    (key_sum, value_sum), query_out = lax.scan(one_block, (empty, empty), jnp.arange(block_count, dtype=jnp.int32))
    query_grad = query_out.reshape(GROUPS, GROUP_TOKENS, HEADS * HEAD_DIM)
    key_grad = (key_sum * key_factor[:, None, :]).astype(jnp.bfloat16).reshape(GROUPS, GROUP_TOKENS, kv_width)
    value_grad = (value_sum * value_factor[:, None, :]).astype(jnp.bfloat16).reshape(GROUPS, GROUP_TOKENS, kv_width)
    return (query_grad, key_grad, value_grad)
```

```python
import functools

import jax
import jax.numpy as jnp
from jax import lax
from jax.experimental import pallas as pl
from jax.experimental.pallas import tpu as pltpu
from jax.sharding import PartitionSpec as P

HEAD_DIM = 128
STEPS = 4
NT = (((1,), (1,)), ((), ()))
NN = (((1,), (0,)), ((), ()))
LOG2E = 1.4426950408889634


def dot(a, b, dims):
    return lax.dot_general(a, b, dims, preferred_element_type=jnp.float32)


def power(e):
    return jnp.where(e > 0, 2.0, jnp.where(e < 0, 0.5, 1.0)).astype(jnp.float32)


def kernel(
    inner_count, outer_count, kv_count, group_size, length,
    mask_ref, exp_ref, k_ref, v_ref, q_ref, do_ref, o_ref,
    dq_ref, dk_ref, dv_ref,
    kv, kt, delta, acc, own, part, comb, rin,
    fwd_send, fwd_recv, bwd_send, bwd_recv,
):
    scale = HEAD_DIM ** (-0.5)
    b = lax.axis_index("outer") * inner_count + lax.axis_index("inner")
    c = lax.rem(lax.axis_index("inner"), 2)
    total = inner_count * outer_count
    partner = b + 1 - 2 * c

    def device(t):
        return {"outer": t // inner_count, "inner": lax.rem(t, inner_count)}

    def remote(src, dst, send, recv, t):
        return pltpu.make_async_remote_copy(
            src_ref=src, dst_ref=dst, send_sem=send, recv_sem=recv,
            device_id=device(t), device_id_type=pl.DeviceIdType.MESH,
        )

    far_up = b + 3 * c
    neighbours = [
        (partner, None),
        (b + 2, b + 2 < total),
        (b - 2, b >= 2),
        (b - 3 + 6 * c, jnp.logical_and(b - 3 + 6 * c >= 0, b - 3 + 6 * c < total)),
    ]
    barrier = pltpu.get_barrier_semaphore()

    def guarded(cond, fn):
        if cond is None:
            fn()
        else:
            pl.when(cond)(fn)

    for t, cond in neighbours:
        guarded(cond, lambda t=t: pl.semaphore_signal(
            barrier, inc=1, device_id=device(t), device_id_type=pl.DeviceIdType.MESH))

    for g in range(kv_count):
        cols = pl.ds(g * HEAD_DIM, HEAD_DIM)
        kf = power(exp_ref[0, 0, g])
        vf = power(exp_ref[0, 0, kv_count + g])
        kv[g, 0, 0] = (k_ref[0, :, cols].astype(jnp.float32) * kf).astype(jnp.bfloat16)
        kv[g, 1, 0] = (v_ref[0, :, cols].astype(jnp.float32) * vf).astype(jnp.bfloat16)

    pl.semaphore_wait(barrier, sum(
        (1 if cond is None else cond.astype(jnp.int32)) for _, cond in neighbours))

    def fwd_far(g):
        return remote(kv.at[g, :, 0], kv.at[g, :, 2], fwd_send.at[0, g], fwd_recv.at[2, g], b + 2)

    def fwd_second(g):
        slot = 1 + 2 * c
        return remote(kv.at[g, :, 0], kv.at[g, :, slot], fwd_send.at[1, g], fwd_recv.at[slot, g], b + 1 + 2 * c)

    def fwd_pass(g):
        slot = 3 - 2 * c
        return remote(kv.at[g, :, 2], kv.at[g, :, slot], fwd_send.at[2, g], fwd_recv.at[slot, g], partner)

    def fwd_wait(s, g):
        remote(kv.at[g, :, s], kv.at[g, :, s], fwd_send.at[0, g], fwd_recv.at[s, g], partner).wait_recv()

    has_far = b + 2 < total
    has_second = b + 1 + 2 * c < total
    has_prev = b >= 2
    has_back = b - 3 + 2 * c >= 0
    has_final = b + 1 + 2 * c < total

    for g in range(kv_count):
        pl.when(has_far)(lambda g=g: fwd_far(g).start())
        pl.when(has_second)(lambda g=g: fwd_second(g).start())

    for s in range(1, STEPS):
        @pl.when(b < s)
        def _():
            for g in range(kv_count):
                for i in range(2):
                    kv[g, i, s] = jnp.zeros((length, HEAD_DIM), jnp.bfloat16)

    heads = kv_count * group_size

    @pl.loop(0, heads)
    def _(h):
        cols = pl.ds(pl.multiple_of(h * HEAD_DIM, HEAD_DIM), HEAD_DIM)
        prod = do_ref[0, :, cols].astype(jnp.float32) * o_ref[0, :, cols].astype(jnp.float32)
        high = prod.astype(jnp.bfloat16)
        low = (prod - high.astype(jnp.float32)).astype(jnp.bfloat16)
        ones = jnp.ones((16, HEAD_DIM), jnp.bfloat16)
        delta[h] = dot(ones, high, NT) + dot(ones, low, NT)

    bias = [None] + [
        jnp.where(jnp.logical_and(b >= s, mask_ref[0, 0, s - 1] == 1), 0.0, -1e30).astype(jnp.float32)
        for s in range(1, STEPS)
    ]

    def compute(g, first, count):
        @pl.loop(first, first + count)
        def _(j):
            h = g * group_size + j
            cols = pl.ds(pl.multiple_of(h * HEAD_DIM, HEAD_DIM), HEAD_DIM)
            qh = q_ref[0, :, cols]
            doh = do_ref[0, :, cols]
            scores = []
            top = None
            for s in range(STEPS):
                x = dot(kv[g, 0, s], qh, NT)
                if s == 0:
                    u = lax.broadcasted_iota(jnp.int32, (length, length), 0)
                    t = lax.broadcasted_iota(jnp.int32, (length, length), 1)
                    x = jnp.where(u <= t, x, -1e30)
                else:
                    x = x + bias[s]
                scores.append(x)
                m = jnp.max(x, 0, keepdims=True)
                top = m if top is None else jnp.maximum(top, m)
            top = top * (scale * LOG2E)
            exps = []
            norm = None
            for s in range(STEPS):
                e = jnp.exp2(scores[s] * (scale * LOG2E) - top)
                exps.append(e)
                n = jnp.sum(e, 0, keepdims=True)
                norm = n if norm is None else norm + n
            inv = 1.0 / norm
            d = delta[h, 0:1, :]
            dqt = None
            for s in range(STEPS):
                p = exps[s] * inv
                dp = dot(kv[g, 1, s], doh, NT)
                ds = (p * (dp - d)).astype(jnp.bfloat16)
                term = dot(kt[:, s * length:(s + 1) * length], ds, NN)
                dqt = term if dqt is None else dqt + term
                acc[0, s] += dot(ds, qh, NN)
                acc[1, s] += dot(p.astype(jnp.bfloat16), doh, NN)
            dq_ref[0, :, cols] = (dqt.T * scale).astype(jnp.bfloat16)

    def bwd_combine(g):
        return remote(part.at[g, 2 * c], rin.at[g, 0], bwd_send.at[0, g], bwd_recv.at[0, g], partner)

    def bwd_far(g):
        return remote(comb.at[g], rin.at[g, 1], bwd_send.at[1, g], bwd_recv.at[1, g], b - 2)

    def bwd_second(g):
        return remote(part.at[g, 2 - 2 * c], rin.at[g, 2], bwd_send.at[2, g], bwd_recv.at[2, g], b - 3 + 2 * c)

    def bwd_wait(slot, g):
        remote(rin.at[g, slot], rin.at[g, slot], bwd_send.at[0, g], bwd_recv.at[slot, g], partner).wait_recv()

    def take(g):
        @pl.when(has_prev)
        def _():
            bwd_wait(0, g)
            comb[g] = (part[g, 1].astype(jnp.float32) + rin[g, 0].astype(jnp.float32)).astype(jnp.bfloat16)
            bwd_far(g).start()

    def pass_on(g):
        @pl.when(has_prev)
        def _():
            fwd_wait(2, g)
            fwd_pass(g).start()

    half = group_size // 2
    pass_on(0)
    for g in range(kv_count):
        pl.when(b >= 1)(lambda g=g: fwd_wait(1, g))
        pl.when(b >= 3)(lambda g=g: fwd_wait(3, g))
        for s in range(STEPS):
            kt[:, s * length:(s + 1) * length] = kv[g, 0, s].T
        acc[...] = jnp.zeros_like(acc)
        compute(g, 0, half)
        if g + 1 < kv_count:
            pass_on(g + 1)
        if g > 0:
            take(g - 1)
        compute(g, half, group_size - half)
        own[g] = acc[:, 0]
        for s in range(1, STEPS):
            part[g, s - 1] = acc[:, s].astype(jnp.bfloat16)
        pl.when(has_prev)(lambda g=g: bwd_combine(g).start())
        pl.when(has_back)(lambda g=g: bwd_second(g).start())
    take(kv_count - 1)

    for g in range(kv_count):
        @pl.when(has_far)
        def _():
            bwd_wait(1, g)
            own[g] += rin[g, 1].astype(jnp.float32)

        @pl.when(has_final)
        def _():
            bwd_wait(2, g)
            own[g] += rin[g, 2].astype(jnp.float32)

        cols = pl.ds(g * HEAD_DIM, HEAD_DIM)
        kf = power(exp_ref[0, 0, g]) * scale
        vf = power(exp_ref[0, 0, kv_count + g])
        dk_ref[0, :, cols] = (own[g, 0] * kf).astype(jnp.bfloat16)
        dv_ref[0, :, cols] = (own[g, 1] * vf).astype(jnp.bfloat16)

    for g in range(kv_count):
        @pl.when(has_far)
        def _():
            fwd_far(g).wait_send()

        @pl.when(has_second)
        def _():
            fwd_second(g).wait_send()

        @pl.when(has_prev)
        def _():
            fwd_pass(g).wait_send()
            bwd_combine(g).wait_send()
            bwd_far(g).wait_send()

        @pl.when(has_back)
        def _():
            bwd_second(g).wait_send()


def body(mesh, queries, keys, values, out_grad, attn_out, block_mask, scale_exponents):
    length = queries.shape[1]
    kv_width = keys.shape[2]
    kv_count = kv_width // HEAD_DIM
    group_size = queries.shape[2] // kv_width
    heads = kv_count * group_size
    bf16, f32 = jnp.bfloat16, jnp.float32
    vmem = pl.BlockSpec(memory_space=pltpu.VMEM)
    smem = pl.BlockSpec(memory_space=pltpu.SMEM)
    block = (length, HEAD_DIM)
    return pl.pallas_call(
        functools.partial(
            kernel, mesh.shape["inner"], mesh.shape["outer"], kv_count, group_size, length
        ),
        out_shape=(
            jax.ShapeDtypeStruct(queries.shape, bf16),
            jax.ShapeDtypeStruct(keys.shape, bf16),
            jax.ShapeDtypeStruct(values.shape, bf16),
        ),
        in_specs=[smem, smem] + [vmem] * 5,
        out_specs=(vmem, vmem, vmem),
        scratch_shapes=[
            pltpu.VMEM((kv_count, 2, STEPS) + block, bf16),
            pltpu.VMEM((HEAD_DIM, STEPS * length), bf16),
            pltpu.VMEM((heads, 16, length), f32),
            pltpu.VMEM((2, STEPS) + block, f32),
            pltpu.VMEM((kv_count, 2) + block, f32),
            pltpu.VMEM((kv_count, STEPS - 1, 2) + block, bf16),
            pltpu.VMEM((kv_count, 2) + block, bf16),
            pltpu.VMEM((kv_count, 3, 2) + block, bf16),
            pltpu.SemaphoreType.DMA((3, kv_count)),
            pltpu.SemaphoreType.DMA((STEPS, kv_count)),
            pltpu.SemaphoreType.DMA((3, kv_count)),
            pltpu.SemaphoreType.DMA((3, kv_count)),
        ],
        compiler_params=pltpu.CompilerParams(
            collective_id=0, has_side_effects=True, vmem_limit_bytes=48 * 1024 * 1024
        ),
    )(block_mask, scale_exponents, keys, values, queries, out_grad, attn_out)


def solution(mesh):
    spec = P(("grp", "outer"), "inner", None)
    return jax.shard_map(
        functools.partial(body, mesh),
        mesh=mesh,
        in_specs=(spec,) * 7,
        out_specs=(spec,) * 3,
        check_vma=False,
    )
```

```python
import functools

import jax
import jax.numpy as jnp
from jax import lax
from jax.experimental import pallas as pl
from jax.experimental.pallas import tpu as pltpu
from jax.sharding import PartitionSpec as P

HEAD_DIM = 128
STEPS = 4
NT = (((1,), (1,)), ((), ()))
NN = (((1,), (0,)), ((), ()))
LOG2E = 1.4426950408889634


def dot(a, b, dims):
    return lax.dot_general(a, b, dims, preferred_element_type=jnp.float32)


def power(e):
    return jnp.where(e > 0, 2.0, jnp.where(e < 0, 0.5, 1.0)).astype(jnp.float32)


def kernel(
    inner_count, outer_count, kv_count, group_size, length,
    *refs,
):
    sources = refs[:7]
    dq_ref, dk_ref, dv_ref = refs[7:10]
    kv, kt, delta, weights, tall, own, part, comb, rin = refs[10:19]
    fwd_send, fwd_recv, bwd_send, bwd_recv, load_sem = refs[19:24]
    staged = refs[24:]
    mask_ref, exp_ref, k_ref, v_ref, q_ref, do_ref, o_ref = staged
    loads = [pltpu.make_async_copy(a, z, load_sem.at[i]) for i, (a, z) in enumerate(zip(sources, staged))]
    for load in loads:
        load.start()
    scale = HEAD_DIM ** (-0.5)
    b = lax.axis_index("outer") * inner_count + lax.axis_index("inner")
    c = lax.rem(lax.axis_index("inner"), 2)
    total = inner_count * outer_count
    partner = b + 1 - 2 * c

    def device(t):
        return {"outer": t // inner_count, "inner": lax.rem(t, inner_count)}

    def remote(src, dst, send, recv, t):
        return pltpu.make_async_remote_copy(
            src_ref=src, dst_ref=dst, send_sem=send, recv_sem=recv,
            device_id=device(t), device_id_type=pl.DeviceIdType.MESH,
        )

    neighbours = [
        (partner, None),
        (b + 2, b + 2 < total),
        (b - 2, b >= 2),
        (b - 3 + 6 * c, jnp.logical_and(b - 3 + 6 * c >= 0, b - 3 + 6 * c < total)),
    ]
    barrier = pltpu.get_barrier_semaphore()

    def guarded(cond, fn):
        if cond is None:
            fn()
        else:
            pl.when(cond)(fn)

    for t, cond in neighbours:
        guarded(cond, lambda t=t: pl.semaphore_signal(
            barrier, inc=1, device_id=device(t), device_id_type=pl.DeviceIdType.MESH))

    for load in loads[:4]:
        load.wait()
    for g in range(kv_count):
        cols = pl.ds(g * HEAD_DIM, HEAD_DIM)
        kf = power(exp_ref[0, :, g:g + 1])
        vf = power(exp_ref[0, :, kv_count + g:kv_count + g + 1])
        kv[g, 0, 0] = (k_ref[0, :, cols].astype(jnp.float32) * kf).astype(jnp.bfloat16)
        kv[g, 1, 0] = (v_ref[0, :, cols].astype(jnp.float32) * vf).astype(jnp.bfloat16)

    pl.semaphore_wait(barrier, sum(
        (1 if cond is None else cond.astype(jnp.int32)) for _, cond in neighbours))

    def fwd_far(g):
        return remote(kv.at[g, :, 0], kv.at[g, :, 2], fwd_send.at[0, g], fwd_recv.at[2, g], b + 2)

    def fwd_second(g):
        slot = 1 + 2 * c
        return remote(kv.at[g, :, 0], kv.at[g, :, slot], fwd_send.at[1, g], fwd_recv.at[slot, g], b + 1 + 2 * c)

    def fwd_pass(g):
        slot = 3 - 2 * c
        return remote(kv.at[g, :, 2], kv.at[g, :, slot], fwd_send.at[2, g], fwd_recv.at[slot, g], partner)

    def fwd_wait(s, g):
        remote(kv.at[g, :, s], kv.at[g, :, s], fwd_send.at[0, g], fwd_recv.at[s, g], partner).wait_recv()

    has_far = b + 2 < total
    has_second = b + 1 + 2 * c < total
    has_prev = b >= 2
    has_back = b - 3 + 2 * c >= 0
    has_final = b + 1 + 2 * c < total

    def send(g):
        pl.when(has_far)(lambda: fwd_far(g).start())
        pl.when(has_second)(lambda: fwd_second(g).start())

    send(0)

    for s in range(1, STEPS):
        @pl.when(b < s)
        def _():
            for g in range(kv_count):
                for i in range(2):
                    kv[g, i, s] = jnp.zeros((length, HEAD_DIM), jnp.bfloat16)

    heads = kv_count * group_size
    for load in loads[4:]:
        load.wait()

    @pl.loop(0, heads)
    def _(h):
        cols = pl.ds(pl.multiple_of(h * HEAD_DIM, HEAD_DIM), HEAD_DIM)
        prod = do_ref[0, :, cols].astype(jnp.float32) * o_ref[0, :, cols].astype(jnp.float32)
        high = prod.astype(jnp.bfloat16)
        low = (prod - high.astype(jnp.float32)).astype(jnp.bfloat16)
        ones = jnp.ones((16, HEAD_DIM), jnp.bfloat16)
        delta[h] = dot(ones, high, NT) + dot(ones, low, NT)

    bias = [None] + [
        jnp.where(mask_ref[0, :, s - 1:s] == 1, 0.0, -1e30).astype(jnp.float32)
        + jnp.where(b >= s, 0.0, -1e30).astype(jnp.float32)
        for s in range(1, STEPS)
    ]

    def compute(g, first, count):
        @pl.loop(first, first + count, unroll=2)
        def _(j):
            h = g * group_size + j
            cols = pl.ds(pl.multiple_of(h * HEAD_DIM, HEAD_DIM), HEAD_DIM)
            qh = q_ref[0, :, cols]
            doh = do_ref[0, :, cols]
            rows = pl.ds(pl.multiple_of(j * length, length), length)
            tall[0, rows, :] = qh
            tall[1, rows, :] = doh
            scores = []
            top = None
            for s in range(STEPS):
                x = dot(kv[g, 0, s], qh, NT)
                if s == 0:
                    u = lax.broadcasted_iota(jnp.int32, (length, length), 0)
                    t = lax.broadcasted_iota(jnp.int32, (length, length), 1)
                    x = jnp.where(u <= t, x, -1e30)
                else:
                    x = x + bias[s]
                scores.append(x)
                m = jnp.max(x, 0, keepdims=True)
                top = m if top is None else jnp.maximum(top, m)
            top = top * (scale * LOG2E)
            exps = []
            norm = None
            for s in range(STEPS):
                e = jnp.exp2(scores[s] * (scale * LOG2E) - top)
                exps.append(e)
                n = jnp.sum(e, 0, keepdims=True)
                norm = n if norm is None else norm + n
            inv = 1.0 / norm
            d = delta[h, 0:1, :]
            dqt = None
            for s in range(STEPS):
                p = exps[s] * inv
                dp = dot(kv[g, 1, s], doh, NT)
                ds = (p * (dp - d)).astype(jnp.bfloat16)
                term = dot(kt[:, s * length:(s + 1) * length], ds, NN)
                dqt = term if dqt is None else dqt + term
                wide = pl.ds(pl.multiple_of(j * length, length), length)
                weights[0, s, :, wide] = ds
                weights[1, s, :, wide] = p.astype(jnp.bfloat16)
            dq_ref[0, :, cols] = (dqt.T * scale).astype(jnp.bfloat16)

    def bwd_combine(g):
        return remote(part.at[g, 2 * c], rin.at[g, 0], bwd_send.at[0, g], bwd_recv.at[0, g], partner)

    def bwd_far(g):
        return remote(comb.at[g], rin.at[g, 1], bwd_send.at[1, g], bwd_recv.at[1, g], b - 2)

    def bwd_second(g):
        return remote(part.at[g, 2 - 2 * c], rin.at[g, 2], bwd_send.at[2, g], bwd_recv.at[2, g], b - 3 + 2 * c)

    def bwd_wait(slot, g):
        remote(rin.at[g, slot], rin.at[g, slot], bwd_send.at[0, g], bwd_recv.at[slot, g], partner).wait_recv()

    def take(g):
        @pl.when(has_prev)
        def _():
            bwd_wait(0, g)
            comb[g] = (part[g, 1].astype(jnp.float32) + rin[g, 0].astype(jnp.float32)).astype(jnp.bfloat16)
            bwd_far(g).start()

    def pass_on(g):
        @pl.when(has_prev)
        def _():
            fwd_wait(2, g)
            fwd_pass(g).start()

    half = group_size // 2
    send(1)
    pass_on(0)
    for g in range(2, kv_count):
        send(g)
    for g in range(kv_count):
        pl.when(b >= 1)(lambda g=g: fwd_wait(1, g))
        pl.when(b >= 3)(lambda g=g: fwd_wait(3, g))
        for s in range(STEPS):
            kt[:, s * length:(s + 1) * length] = kv[g, 0, s].T
        compute(g, 0, half)
        if g + 1 < kv_count:
            pass_on(g + 1)
        if g > 0:
            take(g - 1)
        compute(g, half, group_size - half)
        for s in (3, 1, 2, 0):
            for i in range(2):
                x = dot(weights[i, s], tall[i], NN)
                if s == 0:
                    own[g, i] = x
                else:
                    part[g, s - 1, i] = x.astype(jnp.bfloat16)
        pl.when(has_prev)(lambda g=g: bwd_combine(g).start())
        pl.when(has_back)(lambda g=g: bwd_second(g).start())
    take(kv_count - 1)

    for g in range(kv_count):
        @pl.when(has_far)
        def _():
            bwd_wait(1, g)
            own[g] += rin[g, 1].astype(jnp.float32)

        @pl.when(has_final)
        def _():
            bwd_wait(2, g)
            own[g] += rin[g, 2].astype(jnp.float32)

        cols = pl.ds(g * HEAD_DIM, HEAD_DIM)
        kf = power(exp_ref[0, :, g:g + 1]) * scale
        vf = power(exp_ref[0, :, kv_count + g:kv_count + g + 1])
        dk_ref[0, :, cols] = (own[g, 0] * kf).astype(jnp.bfloat16)
        dv_ref[0, :, cols] = (own[g, 1] * vf).astype(jnp.bfloat16)

    for g in range(kv_count):
        @pl.when(has_far)
        def _():
            fwd_far(g).wait_send()

        @pl.when(has_second)
        def _():
            fwd_second(g).wait_send()

        @pl.when(has_prev)
        def _():
            fwd_pass(g).wait_send()
            bwd_combine(g).wait_send()
            bwd_far(g).wait_send()

        @pl.when(has_back)
        def _():
            bwd_second(g).wait_send()


def write_out(*refs):
    sems = refs[6]
    copies = [pltpu.make_async_copy(refs[i], refs[3 + i], sems.at[i]) for i in range(3)]
    for copy in copies:
        copy.start()
    for copy in copies:
        copy.wait()


def body(mesh, queries, keys, values, out_grad, attn_out, block_mask, scale_exponents):
    length = queries.shape[1]
    kv_width = keys.shape[2]
    kv_count = kv_width // HEAD_DIM
    group_size = queries.shape[2] // kv_width
    heads = kv_count * group_size
    bf16, f32 = jnp.bfloat16, jnp.float32
    vmem = pl.BlockSpec(memory_space=pltpu.VMEM)
    anywhere = pl.BlockSpec(memory_space=pl.ANY)
    arguments = (block_mask, scale_exponents, keys, values, queries, out_grad, attn_out)
    block = (length, HEAD_DIM)
    grads = pl.pallas_call(
        functools.partial(
            kernel, mesh.shape["inner"], mesh.shape["outer"], kv_count, group_size, length
        ),
        out_shape=(
            jax.ShapeDtypeStruct(queries.shape, bf16),
            jax.ShapeDtypeStruct(keys.shape, bf16),
            jax.ShapeDtypeStruct(values.shape, bf16),
        ),
        in_specs=[pl.BlockSpec(memory_space=pltpu.HBM)] * 7,
        out_specs=(vmem, vmem, vmem),
        scratch_shapes=[
            pltpu.VMEM((kv_count, 2, STEPS) + block, bf16),
            pltpu.VMEM((HEAD_DIM, STEPS * length), bf16),
            pltpu.VMEM((heads, 16, length), f32),
            pltpu.VMEM((2, STEPS, length, group_size * length), bf16),
            pltpu.VMEM((2, group_size * length, HEAD_DIM), bf16),
            pltpu.VMEM((kv_count, 2) + block, f32),
            pltpu.VMEM((kv_count, STEPS - 1, 2) + block, bf16),
            pltpu.VMEM((kv_count, 2) + block, bf16),
            pltpu.VMEM((kv_count, 3, 2) + block, bf16),
            pltpu.SemaphoreType.DMA((3, kv_count)),
            pltpu.SemaphoreType.DMA((STEPS, kv_count)),
            pltpu.SemaphoreType.DMA((3, kv_count)),
            pltpu.SemaphoreType.DMA((3, kv_count)),
            pltpu.SemaphoreType.DMA((7,)),
        ] + [pltpu.VMEM(x.shape, x.dtype) for x in arguments],
        compiler_params=pltpu.CompilerParams(
            collective_id=0, has_side_effects=True, vmem_limit_bytes=63 * 1024 * 1024
        ),
    )(*arguments)
    return pl.pallas_call(
        write_out,
        out_shape=tuple(jax.ShapeDtypeStruct(x.shape, x.dtype) for x in grads),
        in_specs=[anywhere] * 3,
        out_specs=(anywhere,) * 3,
        scratch_shapes=[pltpu.SemaphoreType.DMA((3,))],
        compiler_params=pltpu.CompilerParams(vmem_limit_bytes=63 * 1024 * 1024),
    )(*grads)


def solution(mesh):
    spec = P(("grp", "outer"), "inner", None)
    return jax.shard_map(
        functools.partial(body, mesh),
        mesh=mesh,
        in_specs=(spec,) * 7,
        out_specs=(spec,) * 3,
        check_vma=False,
    )
```
